32 devices in a mesh: groups: 2 (over y), ctx: 16 (over z, x, core).
Axes of the slice: x: 2, y: 2, z: 4, core: 2. Of those that a mesh axis runs over, the one named last changes fastest.
Arguments:
- query_rows: bfloat16 [8192, 4096], P(('groups', 'ctx')), parts along dimension 0, may hold values from -6 to 6
- key_rows: bfloat16 [8192, 4096], P(('groups', 'ctx')), parts along dimension 0, may hold values from -6 to 6
- value_rows: bfloat16 [8192, 4096], P(('groups', 'ctx')), parts along dimension 0, may hold values from -6 to 6
- conv_taps: float32 [2, 4, 4096], replicated, may hold values from -3 to 3
- level_table: float32 [64, 12, 32], replicated, may hold values from 0.2 to 2
- table_index: int32 [8192], P(('groups', 'ctx')), parts along dimension 0, may hold values from 0 to 63
- level_columns: int32 [32, 12], P(('groups', 'ctx')), parts along dimension 0, may hold values from 0 to 11
Outputs:
- attended: bfloat16 [8192, 4096], P(('groups', 'ctx')), parts along dimension 0
The draws below stay inside these ranges and needn't reach their ends.
There are 2 independent parts, one for each index of `groups`. The reference program is written for one: setup_inputs(seed, part) draws one part's arguments, and reference() takes and returns one part's arrays. A program takes and returns all parts, laid end to end along the dimension named above; an argument that names none is the same for every part. Nothing has to cross between parts.
All inputs are finite; a program needn't handle non-finite values.
Results may differ from the reference program's by a relative error of at most 0.0054.
Values may be sent and summed in bfloat16 or wider, within the bound.
A program may use at most 128 MiB of HBM per device.

```python
import math
import jax
import jax.numpy as jnp
from jax import lax

HEAD_COUNT = 32
HEAD_DIM = 128
BLOCK_LEN = 256
TAP_COUNT = 4
LEVELS = 12
TABLE_ROWS = 64
BLOCKS = 16
TOKENS = 4096
CHANNELS = 4096


def place_ends(values, own_key, smallest, largest):
    spot = [jax.random.randint(jax.random.fold_in(own_key, axis), (), 0, length) for axis, length in enumerate(values.shape)]
    widest = values.shape.index(max(values.shape))
    beside = spot[:widest] + [(spot[widest] + 1) % values.shape[widest]] + spot[widest + 1:]
    return values.at[tuple(spot)].set(smallest).at[tuple(beside)].set(largest)


def level_of(key, dims, cuts, least, high):
    def one(position, blocks):
        steps = jax.random.uniform(jax.random.fold_in(jax.random.fold_in(key, 6), position), (blocks,), jnp.float32, least / len(cuts), high / len(cuts))
        return jnp.repeat(jnp.exp(steps), dims[position] // blocks).reshape((-1,) + (1,) * (len(dims) - position - 1))

    loudness = one(*cuts[0])
    for cut in cuts[1:]:
        loudness = loudness * one(*cut)
    return loudness


def bell_draw(stream_key, dims, width, reach, cuts=(), held_as=jnp.bfloat16):
    gain = level_of(stream_key, dims, cuts, -0.22, 0.18) if cuts else 1.0
    drawn = jax.random.normal(stream_key, dims, jnp.float32) * width * gain
    return jnp.minimum(jnp.maximum(drawn, -reach), reach).astype(held_as)


def setup_inputs(seed: int = 0, part: int = 0) -> dict:
    splits = jax.random.split(jax.random.key(seed), 8)
    part_keys = jax.random.split(jax.random.fold_in(splits[7], part), 8)
    return {
        "query_rows": bell_draw(part_keys[0], (TOKENS, CHANNELS), 1.0, 6.0, ((0, 16),)),
        "key_rows": bell_draw(part_keys[1], (TOKENS, CHANNELS), 1.0, 6.0, ((0, 16),)),
        "value_rows": bell_draw(part_keys[2], (TOKENS, CHANNELS), 1.0, 6.0, ((0, 16),)),
        "conv_taps": bell_draw(splits[3], (2, TAP_COUNT, CHANNELS), TAP_COUNT ** -0.5, 3.0, (), jnp.float32),
        "level_table": jnp.clip(jnp.exp(jax.random.uniform(splits[4], (TABLE_ROWS, LEVELS, HEAD_COUNT), jnp.float32, math.log(0.2), math.log(2.0))), 0.2, 2.0),
        "table_index": place_ends(jax.random.randint(part_keys[5], (TOKENS,), 0, TABLE_ROWS), jax.random.fold_in(part_keys[5], 1), 0, TABLE_ROWS - 1).astype(jnp.int32),
        "level_columns": place_ends(jax.random.randint(part_keys[6], (BLOCKS, LEVELS), 0, LEVELS), jax.random.fold_in(part_keys[6], 1), 0, LEVELS - 1).astype(jnp.int32),
    }


def to_half(values):
    return lax.optimization_barrier(values.astype(jnp.bfloat16))

def conv_rows(padded_rows, tap_weights, row_count):
    summed = jnp.zeros((row_count, padded_rows.shape[1]), jnp.float32)
    for offset in range(tap_weights.shape[0]):
        summed = summed + tap_weights[offset] * padded_rows[offset:offset + row_count].astype(jnp.float32)
    return to_half(jax.nn.silu(summed))

def level_scales(levels, block_len, head_dim):
    inv_root = 1.0 / math.sqrt(head_dim)
    factors = [inv_root / math.sqrt(block_len)]
    for level_pos in range(1, levels):
        factors.append(inv_root / math.sqrt(block_len * 2 ** (level_pos - 1)))
    return jnp.array(factors, jnp.float32)

def reference(query_rows, key_rows, value_rows, conv_taps, level_table, table_index, level_columns):
    rim_len = TAP_COUNT - 1

    def padded(row_contents):
        return jnp.concatenate([jnp.zeros((rim_len, CHANNELS), jnp.bfloat16), row_contents], axis=0)
    query_conv = conv_rows(padded(query_rows), conv_taps[0], TOKENS)
    key_conv = conv_rows(padded(key_rows), conv_taps[1], TOKENS)
    query_blocks = query_conv.reshape(BLOCKS, BLOCK_LEN, HEAD_COUNT, HEAD_DIM)
    key_blocks = key_conv.reshape(BLOCKS, BLOCK_LEN, HEAD_COUNT, HEAD_DIM)
    value_blocks = value_rows.reshape(BLOCKS, BLOCK_LEN, HEAD_COUNT, HEAD_DIM)
    selected_entries = level_table[table_index].reshape(BLOCKS, BLOCK_LEN, LEVELS, HEAD_COUNT)
    block_ids = jnp.arange(BLOCKS, dtype=jnp.int32)[:, None, None]
    token_ids = jnp.arange(BLOCK_LEN, dtype=jnp.int32)[None, :, None]
    mixing_weights = selected_entries[block_ids, token_ids, level_columns[:, None, :]]
    mixing_weights = mixing_weights * level_scales(LEVELS, BLOCK_LEN, HEAD_DIM)[None, None, :, None]
    causal = jnp.arange(BLOCK_LEN)[:, None] >= jnp.arange(BLOCK_LEN)[None, :]

    def block_attend(block_items):
        query_one, key_one, value_one = block_items
        scores = jnp.einsum('lhd,shd->hls', query_one.astype(jnp.float32), key_one.astype(jnp.float32))
        scores = to_half(jnp.where(causal[None], scores, 0.0))
        return jnp.einsum('hls,she->lhe', scores.astype(jnp.float32), value_one.astype(jnp.float32))
    local_out = lax.map(block_attend, (query_blocks, key_blocks, value_blocks))
    output = local_out * mixing_weights[:, :, 0, :, None]
    states = jnp.einsum('clhd,clhe->chde', key_blocks.astype(jnp.float32), value_blocks.astype(jnp.float32))
    block_sum = states
    for bit_pos in range(BLOCKS.bit_length() - 1):
        pair_count = BLOCKS >> bit_pos + 1
        half_span = 1 << bit_pos
        grouped = block_sum.reshape(pair_count, 2, HEAD_COUNT, HEAD_DIM, HEAD_DIM)
        lower_half = to_half(grouped[:, 0])
        upper_query = query_blocks.reshape(pair_count, 2, half_span, BLOCK_LEN, HEAD_COUNT, HEAD_DIM)[:, 1]
        level_read = jnp.einsum('prlhd,phde->prlhe', upper_query.astype(jnp.float32), lower_half.astype(jnp.float32))
        level_weight = mixing_weights.reshape(pair_count, 2, half_span, BLOCK_LEN, LEVELS, HEAD_COUNT)[:, 1, :, :, bit_pos + 1]
        shaped = output.reshape(pair_count, 2, half_span, BLOCK_LEN, HEAD_COUNT, HEAD_DIM)
        shaped = shaped.at[:, 1].add(level_read * level_weight[..., None])
        output = shaped.reshape(BLOCKS, BLOCK_LEN, HEAD_COUNT, HEAD_DIM)
        block_sum = grouped[:, 0] + grouped[:, 1]
    return output.reshape(TOKENS, CHANNELS).astype(jnp.bfloat16)
```

```python
import functools
import math

import jax
import jax.numpy as jnp
from jax import lax
from jax.experimental import pallas as pl
from jax.experimental.pallas import tpu as pltpu
from jax.sharding import PartitionSpec as P

F32 = jnp.float32
BF16 = jnp.bfloat16
PAD = 16


def level_factors(levels, block_len, head_dim):
    inv_root = 1.0 / math.sqrt(head_dim)
    factors = [inv_root / math.sqrt(block_len)]
    for level_pos in range(1, levels):
        factors.append(inv_root / math.sqrt(block_len * 2 ** (level_pos - 1)))
    return factors


def kernel(
    bits, heads, dim, q_hbm, k_hbm, v_hbm, taps_ref, table_ref, index_ref, cols_ref,
    out_ref, q_v, k_v, v_v, qc, kc, st_f, st_b, half_f, half_b, quart_f, quart_b,
    buck, acc, coef, load_sem, send_sem, recv_sem,
):
    tokens = q_hbm.shape[0]
    n = 2**bits
    group = lax.axis_index("groups")
    pos = lax.axis_index("ctx")
    bit = [(pos // 2**b) % 2 for b in range(bits)]
    partner = [pos + 2**b * (1 - 2 * bit[b]) for b in range(bits)]
    quarter = heads // 4
    half = heads // 2

    loads = [
        pltpu.make_async_copy(src, dst.at[pl.ds(start, tokens)], load_sem.at[i])
        for i, (src, dst, start) in enumerate(((k_hbm, k_v, PAD), (v_hbm, v_v, 0), (q_hbm, q_v, PAD)))
    ]
    for load in loads:
        load.start()

    barrier = pltpu.get_barrier_semaphore()

    def greet(other):
        pl.semaphore_signal(
            barrier, inc=1, device_id=(group, other), device_id_type=pl.DeviceIdType.MESH
        )

    for b in range(bits):
        greet(partner[b])

    @pl.when(pos > 0)
    def _():
        greet(pos - 1)

    @pl.when(pos < n - 1)
    def _():
        greet(pos + 1)

    ends = (pos == 0).astype(jnp.int32) + (pos == n - 1).astype(jnp.int32)
    pl.semaphore_wait(barrier, bits + 2 - ends)

    def remote(i, src, dst, other):
        return pltpu.make_async_remote_copy(
            src_ref=src, dst_ref=dst, send_sem=send_sem.at[i], recv_sem=recv_sem.at[i],
            device_id=(group, other), device_id_type=pl.DeviceIdType.MESH,
        )

    started = []

    def send(copy, when=None):
        started.append((copy, when))
        if when is None:
            copy.start()
        else:
            pl.when(when)(copy.start)

    def wait(copy, when=None):
        if when is None:
            copy.wait_recv()
        else:
            pl.when(when)(copy.wait_recv)

    rims = []
    for i, (src, dst) in enumerate(((k_hbm, k_v), (q_hbm, q_v))):
        rim = remote(i, src.at[pl.ds(tokens - PAD, PAD)], dst.at[pl.ds(0, PAD)], pos + 1)
        send(rim, pos < n - 1)
        rims.append(rim)

    def finish_rim(i, ref):
        wait(rims[i], pos > 0)

        @pl.when(pos == 0)
        def _():
            ref[pl.ds(0, PAD), :] = jnp.zeros((PAD, ref.shape[1]), BF16)

    def lanes(h):
        return pl.ds(pl.multiple_of(h * dim, dim), dim)

    def conv(ref, which, h):
        rows = ref[:, lanes(h)].astype(F32)
        taps = taps_ref[which, :, lanes(h)]
        count = taps.shape[0]
        total = taps[count - 1 : count] * rows[PAD:]
        for back in range(1, count):
            total = total + taps[count - 1 - back : count - back] * pltpu.roll(rows, back, 0)[PAD:]
        return (0.5 * total * (1.0 + jnp.tanh(0.5 * total))).astype(BF16)

    def state_body(h, carry):
        key = conv(k_v, 1, h)
        kc[h] = key
        state = lax.dot_general(
            key, v_v[:, lanes(h)], (((0,), (0,)), ((), ())), preferred_element_type=F32
        )
        st_f[h] = state
        st_b[h] = state.astype(BF16)
        return carry

    own_half = bit[0] * half
    other_half = (1 - bit[0]) * half
    own_quart = own_half + bit[1] * quarter
    other_quart = own_half + (1 - bit[1]) * quarter

    loads[0].wait()
    loads[1].wait()
    finish_rim(0, k_v)
    firsts = [
        other_half + (1 - bit[1]) * quarter, other_half + bit[1] * quarter, other_quart, own_quart
    ]
    pair = []
    for i, first in enumerate(firsts):
        lax.fori_loop(first, first + quarter, state_body, 0)
        heads_i = pl.ds(first, quarter)
        copy = remote(2 + i, st_b.at[heads_i], buck.at[0, heads_i], partner[0])
        send(copy, None if i < 2 else bit[0] == 0)
        pair.append(copy)

    def coefficients():
        table = table_ref[...]
        rows, levels, _ = table.shape
        factors = level_factors(levels, tokens, dim)
        middle = lax.broadcasted_iota(jnp.int32, table.shape, 1)
        head_id = lax.broadcasted_iota(jnp.int32, (heads, heads * 8), 0)
        lane_id = lax.broadcasted_iota(jnp.int32, (heads, heads * 8), 1)
        mixed = jnp.zeros((rows, heads * 8), F32)
        for level in range(bits + 1):
            column = jnp.sum(jnp.where(middle == cols_ref[0, level], table, 0.0), axis=1)
            place = (lane_id == head_id * 8 + level).astype(F32)
            mixed = mixed + jnp.dot(
                column * factors[level], place,
                precision=lax.Precision.HIGHEST, preferred_element_type=F32,
            )
        hot = (lax.broadcasted_iota(jnp.int32, (rows, tokens), 0) == index_ref[...]).astype(F32)
        weights = jnp.dot(
            hot.T, mixed, precision=lax.Precision.HIGHEST, preferred_element_type=F32
        )
        for h in range(heads):
            coef[h] = weights[:, h * 8 : h * 8 + 8]

    coefficients()

    for i in range(2):
        wait(pair[i])

    def half_body(i, carry):
        h = own_half + i
        total = st_f[h] + buck[0, h].astype(F32)
        half_f[i] = total
        half_b[i] = total.astype(BF16)
        return carry

    lax.fori_loop(0, half, half_body, 0)
    shares = []
    for i, (inner, first) in enumerate((
        ((1 - bit[1]) * quarter, other_quart), (bit[1] * quarter, own_quart)
    )):
        copy = remote(
            6 + i, half_b.at[pl.ds(inner, quarter)], buck.at[1, pl.ds(first, quarter)], partner[1]
        )
        send(copy, None if i == 0 else bit[1] == 0)
        shares.append(copy)

    causal = lax.broadcasted_iota(jnp.int32, (tokens, tokens), 0) >= lax.broadcasted_iota(
        jnp.int32, (tokens, tokens), 1
    )

    def local_body(h, carry):
        query = conv(q_v, 0, h)
        qc[h] = query
        score = lax.dot_general(
            query, kc[h], (((1,), (1,)), ((), ())), preferred_element_type=F32
        )
        score = jnp.where(causal, score, 0.0).astype(BF16)
        read = jnp.dot(score, v_v[:, lanes(h)], preferred_element_type=F32)
        acc[h] = read * coef[h][:, 0:1]
        return carry

    def local(part):
        lax.fori_loop(part * quarter, (part + 1) * quarter, local_body, 0)

    loads[2].wait()
    finish_rim(1, q_v)
    local(0)

    wait(shares[0])

    def quart_body(i, carry):
        total = half_f[bit[1] * quarter + i] + buck[1, own_quart + i].astype(F32)
        quart_f[i] = total
        quart_b[0, i] = total.astype(BF16)
        return carry

    lax.fori_loop(0, quarter, quart_body, 0)
    base = 9

    def exchange(b):
        copy = remote(
            base + 3 * (b - 2), quart_b.at[b - 2], buck.at[b, pl.ds(own_quart, quarter)], partner[b]
        )
        send(copy, None if b < bits - 1 else bit[b] == 0)
        return copy

    hops = {2: exchange(2)}

    wait(shares[1], bit[1] == 1)
    over = remote(
        8, buck.at[1, pl.ds(own_half, half)], buck.at[1, pl.ds(own_half, half)], partner[0]
    )
    send(over, bit[1] == 1)
    local(1)

    def gather_x(b):
        quart = buck.at[b, pl.ds(own_quart, quarter)]
        copy = remote(base + 3 * (b - 2) + 1, quart, quart, partner[1])
        send(copy, bit[b] == 1)
        return copy

    def gather_core(b):
        own = buck.at[b, pl.ds(own_half, half)]
        copy = remote(base + 3 * (b - 2) + 2, own, own, partner[0])
        send(copy, bit[b] == 1)
        return copy

    gx = {}
    gc = {}
    for b in range(2, bits):
        wait(hops[b], None if b < bits - 1 else bit[b] == 1)
        gx[b] = gather_x(b)
        if b < bits - 1:

            def more_body(i, carry, b=b):
                total = quart_f[i] + buck[b, own_quart + i].astype(F32)
                quart_f[i] = total
                quart_b[b - 1, i] = total.astype(BF16)
                return carry

            lax.fori_loop(0, quarter, more_body, 0)
            hops[b + 1] = exchange(b + 1)
        if b == 2:
            local(2)
            local(3)
        wait(gx[b], bit[b] == 1)
        gc[b] = gather_core(b)

    def read_level(b):
        def body(h, carry):
            acc[h] += (
                jnp.dot(qc[h], buck[b, h], preferred_element_type=F32) * coef[h][:, b + 1 : b + 2]
            )
            return carry

        @pl.when(bit[b] == 1)
        def _():
            lax.fori_loop(0, heads, body, 0)

    wait(pair[2], bit[0] == 1)
    wait(pair[3], bit[0] == 1)
    read_level(0)
    wait(over, bit[1] == 1)
    read_level(1)
    for b in range(2, bits):
        wait(gc[b], bit[b] == 1)
        read_level(b)

    def out_body(h, carry):
        out_ref[:, lanes(h)] = acc[h].astype(BF16)
        return carry

    lax.fori_loop(0, heads, out_body, 0)

    for copy, when in started:
        if when is None:
            copy.wait_send()
        else:
            pl.when(when)(copy.wait_send)


def on_device(query_rows, key_rows, value_rows, conv_taps, level_table, table_index, level_columns):
    tokens, width = query_rows.shape
    heads = level_table.shape[2]
    dim = width // heads
    bits = lax.axis_size("ctx").bit_length() - 1
    quarter = heads // 4
    vmem = pl.BlockSpec(memory_space=pltpu.VMEM)
    hbm = pl.BlockSpec(memory_space=pl.ANY)
    copies = 9 + 3 * (bits - 2)
    return pl.pallas_call(
        functools.partial(kernel, bits, heads, dim),
        out_shape=jax.ShapeDtypeStruct((tokens, width), BF16),
        in_specs=[hbm, hbm, hbm, vmem, vmem, vmem, pl.BlockSpec(memory_space=pltpu.SMEM)],
        out_specs=vmem,
        scratch_shapes=[
            pltpu.VMEM((PAD + tokens, width), BF16),
            pltpu.VMEM((PAD + tokens, width), BF16),
            pltpu.VMEM((tokens, width), BF16),
            pltpu.VMEM((heads, tokens, dim), BF16),
            pltpu.VMEM((heads, tokens, dim), BF16),
            pltpu.VMEM((heads, dim, dim), F32),
            pltpu.VMEM((heads, dim, dim), BF16),
            pltpu.VMEM((heads // 2, dim, dim), F32),
            pltpu.VMEM((heads // 2, dim, dim), BF16),
            pltpu.VMEM((quarter, dim, dim), F32),
            pltpu.VMEM((bits - 2, quarter, dim, dim), BF16),
            pltpu.VMEM((bits, heads, dim, dim), BF16),
            pltpu.VMEM((heads, tokens, dim), F32),
            pltpu.VMEM((heads, tokens, 8), F32),
            pltpu.SemaphoreType.DMA((3,)),
            pltpu.SemaphoreType.DMA((copies,)),
            pltpu.SemaphoreType.DMA((copies,)),
        ],
        compiler_params=pltpu.CompilerParams(
            collective_id=0, has_side_effects=True, vmem_limit_bytes=56 * 2**20
        ),
    )(
        query_rows, key_rows, value_rows, conv_taps, level_table,
        table_index.reshape(1, tokens), level_columns,
    )


def solution(mesh):
    rows = P(("groups", "ctx"), None)
    return jax.shard_map(
        on_device,
        mesh=mesh,
        in_specs=(rows, rows, rows, P(), P(), P(("groups", "ctx")), rows),
        out_specs=rows,
        check_vma=False,
    )
```

```python
import functools
import math

import jax
import jax.numpy as jnp
from jax import lax
from jax.experimental import pallas as pl
from jax.experimental.pallas import tpu as pltpu
from jax.sharding import PartitionSpec as P

F32 = jnp.float32
BF16 = jnp.bfloat16
PAD = 16


def level_factors(levels, block_len, head_dim):
    inv_root = 1.0 / math.sqrt(head_dim)
    factors = [inv_root / math.sqrt(block_len)]
    for level_pos in range(1, levels):
        factors.append(inv_root / math.sqrt(block_len * 2 ** (level_pos - 1)))
    return factors


def kernel(
    bits, heads, dim, q_hbm, k_hbm, v_hbm, taps_ref, table_ref, index_ref, cols_ref,
    out_ref, q_v, k_v, v_v, qc, kc, st_f, st_b, half_f, half_b, quart_f, quart_b,
    buck, acc, coef, load_sem, send_sem, recv_sem,
):
    tokens = q_hbm.shape[0]
    n = 2**bits
    group = lax.axis_index("groups")
    pos = lax.axis_index("ctx")
    bit = [(pos // 2**b) % 2 for b in range(bits)]
    partner = [pos + 2**b * (1 - 2 * bit[b]) for b in range(bits)]
    quarter = heads // 4
    half = heads // 2

    loads = [
        pltpu.make_async_copy(src, dst.at[pl.ds(start, tokens)], load_sem.at[i])
        for i, (src, dst, start) in enumerate(((k_hbm, k_v, PAD), (v_hbm, v_v, 0), (q_hbm, q_v, PAD)))
    ]
    for load in loads:
        load.start()

    barrier = pltpu.get_barrier_semaphore()

    def greet(other):
        pl.semaphore_signal(
            barrier, inc=1, device_id=(group, other), device_id_type=pl.DeviceIdType.MESH
        )

    for b in range(bits):
        greet(partner[b])

    @pl.when(pos > 0)
    def _():
        greet(pos - 1)

    @pl.when(pos < n - 1)
    def _():
        greet(pos + 1)

    ends = (pos == 0).astype(jnp.int32) + (pos == n - 1).astype(jnp.int32)
    pl.semaphore_wait(barrier, bits + 2 - ends)

    def remote(i, src, dst, other):
        return pltpu.make_async_remote_copy(
            src_ref=src, dst_ref=dst, send_sem=send_sem.at[i], recv_sem=recv_sem.at[i],
            device_id=(group, other), device_id_type=pl.DeviceIdType.MESH,
        )

    started = []

    def send(copy, when=None):
        started.append((copy, when))
        if when is None:
            copy.start()
        else:
            pl.when(when)(copy.start)

    def wait(copy, when=None):
        if when is None:
            copy.wait_recv()
        else:
            pl.when(when)(copy.wait_recv)

    rims = []
    for i, (src, dst) in enumerate(((k_hbm, k_v), (q_hbm, q_v))):
        rim = remote(i, src.at[pl.ds(tokens - PAD, PAD)], dst.at[pl.ds(0, PAD)], pos + 1)
        send(rim, pos < n - 1)
        rims.append(rim)

    def finish_rim(i, ref):
        wait(rims[i], pos > 0)

        @pl.when(pos == 0)
        def _():
            ref[pl.ds(0, PAD), :] = jnp.zeros((PAD, ref.shape[1]), BF16)

    def lanes(h):
        return pl.ds(pl.multiple_of(h * dim, dim), dim)

    def conv(ref, which, h):
        rows = ref[:, lanes(h)].astype(F32)
        taps = taps_ref[which, :, lanes(h)]
        count = taps.shape[0]
        total = taps[count - 1 : count] * rows[PAD:]
        for back in range(1, count):
            total = total + taps[count - 1 - back : count - back] * pltpu.roll(rows, back, 0)[PAD:]
        return (0.5 * total * (1.0 + jnp.tanh(0.5 * total))).astype(BF16)

    def loop(first, count, step, one):
        def body(i, carry):
            stores = [one(first + i * step + u) for u in range(step)]
            for group_of in stores:
                for ref, at, value in group_of:
                    ref[at] = value
            return carry

        lax.fori_loop(0, count // step, body, 0)

    def state_one(h):
        key = conv(k_v, 1, h)
        state = lax.dot_general(
            key, v_v[:, lanes(h)], (((0,), (0,)), ((), ())), preferred_element_type=F32
        )
        return (kc, h, key), (st_f, h, state), (st_b, h, state.astype(BF16))

    own_half = bit[0] * half
    other_half = (1 - bit[0]) * half
    own_quart = own_half + bit[1] * quarter
    other_quart = own_half + (1 - bit[1]) * quarter

    def coefficients():
        table = table_ref[...]
        levels, _, rows = table.shape
        factors = level_factors(levels, tokens, dim)
        head_id = lax.broadcasted_iota(jnp.int32, (heads * 8, heads), 1)
        lane_id = lax.broadcasted_iota(jnp.int32, (heads * 8, heads), 0)
        leading = lax.broadcasted_iota(jnp.int32, table.shape, 0)
        mixed = jnp.zeros((heads * 8, rows), F32)
        for level in range(bits + 1):
            column = jnp.sum(jnp.where(leading == cols_ref[0, level], table, 0.0), axis=0)
            place = (lane_id == head_id * 8 + level).astype(F32)
            mixed = mixed + jnp.dot(
                place, column * factors[level],
                precision=lax.Precision.HIGHEST, preferred_element_type=F32,
            )
        hot = (lax.broadcasted_iota(jnp.int32, (rows, tokens), 0) == index_ref[...]).astype(F32)
        weights = lax.dot_general(
            hot.T, mixed, (((1,), (1,)), ((), ())),
            precision=lax.Precision.HIGHEST, preferred_element_type=F32,
        )
        for h in range(heads):
            coef[h] = weights[:, h * 8 : h * 8 + 8]

    coefficients()
    loads[0].wait()
    loads[1].wait()
    finish_rim(0, k_v)
    firsts = [
        other_half + (1 - bit[1]) * quarter, other_half + bit[1] * quarter, other_quart, own_quart
    ]
    pair = []
    for i, first in enumerate(firsts):
        loop(first, quarter, 2, state_one)
        heads_i = pl.ds(first, quarter)
        copy = remote(2 + i, st_b.at[heads_i], buck.at[0, heads_i], partner[0])
        send(copy, None if i < 2 else bit[0] == 0)
        pair.append(copy)

    for i in range(2):
        wait(pair[i])

    def half_body(i, carry):
        h = own_half + i
        total = st_f[h] + buck[0, h].astype(F32)
        half_f[i] = total
        half_b[i] = total.astype(BF16)
        return carry

    lax.fori_loop(0, half, half_body, 0)
    shares = []
    for i, (inner, first) in enumerate((
        ((1 - bit[1]) * quarter, other_quart), (bit[1] * quarter, own_quart)
    )):
        copy = remote(
            6 + i, half_b.at[pl.ds(inner, quarter)], buck.at[1, pl.ds(first, quarter)], partner[1]
        )
        send(copy, None if i == 0 else bit[1] == 0)
        shares.append(copy)

    causal = lax.broadcasted_iota(jnp.int32, (tokens, tokens), 0) >= lax.broadcasted_iota(
        jnp.int32, (tokens, tokens), 1
    )

    def local_one(h):
        query = conv(q_v, 0, h)
        score = lax.dot_general(
            query, kc[h], (((1,), (1,)), ((), ())), preferred_element_type=F32
        )
        score = jnp.where(causal, score, 0.0).astype(BF16)
        read = jnp.dot(score, v_v[:, lanes(h)], preferred_element_type=F32)
        return (qc, h, query), (acc, h, read * coef[h][:, 0:1])

    def local(part):
        loop(part * quarter, quarter, 2, local_one)

    loads[2].wait()
    finish_rim(1, q_v)
    local(0)
    local(1)

    wait(shares[0])

    def quart_body(i, carry):
        total = half_f[bit[1] * quarter + i] + buck[1, own_quart + i].astype(F32)
        quart_f[i] = total
        quart_b[0, i] = total.astype(BF16)
        return carry

    lax.fori_loop(0, quarter, quart_body, 0)
    base = 9

    def exchange(b):
        copy = remote(
            base + 4 * (b - 2), quart_b.at[b - 2], buck.at[b, pl.ds(own_quart, quarter)], partner[b]
        )
        send(copy, None if b < bits - 1 else bit[b] == 0)
        return copy

    hops = {2: exchange(2)}

    wait(shares[1], bit[1] == 1)
    over = remote(
        8, buck.at[1, pl.ds(own_half, half)], buck.at[1, pl.ds(own_half, half)], partner[0]
    )
    send(over, bit[1] == 1)
    local(2)
    local(3)

    def gather_x(b):
        quart = buck.at[b, pl.ds(own_quart, quarter)]
        copy = remote(base + 4 * (b - 2) + 1, quart, quart, partner[1])
        send(copy, bit[b] == 1)
        return copy

    def gather_core(b, i, first):
        quart = buck.at[b, pl.ds(first, quarter)]
        copy = remote(base + 4 * (b - 2) + 2 + i, quart, quart, partner[0])
        send(copy, bit[b] == 1)
        return copy

    def level_term(b, h):
        read = jnp.dot(qc[h], buck[b, h], preferred_element_type=F32)
        return acc[h] + read * coef[h][:, b + 1 : b + 2]

    def read_level(b):
        @pl.when(bit[b] == 1)
        def _():
            loop(0, heads, 4, lambda h: ((acc, h, level_term(b, h)),))

    last = bits - 1
    for b in range(2, bits):
        wait(hops[b], None if b < last else bit[b] == 1)
        across = gather_x(b)
        near = gather_core(b, 0, own_quart)
        if b < last:

            def more_body(i, carry, b=b):
                total = quart_f[i] + buck[b, own_quart + i].astype(F32)
                quart_f[i] = total
                quart_b[b - 1, i] = total.astype(BF16)
                return carry

            lax.fori_loop(0, quarter, more_body, 0)
            hops[b + 1] = exchange(b + 1)
            if b == 2:
                wait(pair[2], bit[0] == 1)
                wait(pair[3], bit[0] == 1)
                read_level(0)
                wait(over, bit[1] == 1)
                read_level(1)
            wait(across, bit[b] == 1)
            far = gather_core(b, 1, other_quart)
            wait(near, bit[b] == 1)
            wait(far, bit[b] == 1)
            read_level(b)

    def finish(first):
        def out_at(h):
            return (slice(None), lanes(h))

        loop(
            first, quarter, 4,
            lambda h: ((out_ref, out_at(h), level_term(last, h).astype(BF16)),),
        )

    @pl.when(bit[last] == 1)
    def _():
        finish(own_quart)
        near.wait_recv()
        finish(other_half + bit[1] * quarter)
        across.wait_recv()

    far = gather_core(last, 1, other_quart)

    @pl.when(bit[last] == 1)
    def _():
        finish(other_quart)
        far.wait_recv()
        finish(other_half + (1 - bit[1]) * quarter)

    @pl.when(bit[last] == 0)
    def _():
        loop(0, heads, 4, lambda h: ((out_ref, (slice(None), lanes(h)), acc[h].astype(BF16)),))

    for copy, when in started:
        if when is None:
            copy.wait_send()
        else:
            pl.when(when)(copy.wait_send)


def on_device(query_rows, key_rows, value_rows, conv_taps, level_table, table_index, level_columns):
    tokens, width = query_rows.shape
    heads = level_table.shape[2]
    dim = width // heads
    bits = lax.axis_size("ctx").bit_length() - 1
    quarter = heads // 4
    vmem = pl.BlockSpec(memory_space=pltpu.VMEM)
    hbm = pl.BlockSpec(memory_space=pl.ANY)
    copies = 9 + 4 * (bits - 2)
    return pl.pallas_call(
        functools.partial(kernel, bits, heads, dim),
        out_shape=jax.ShapeDtypeStruct((tokens, width), BF16),
        in_specs=[hbm, hbm, hbm, vmem, vmem, vmem, pl.BlockSpec(memory_space=pltpu.SMEM)],
        out_specs=vmem,
        scratch_shapes=[
            pltpu.VMEM((PAD + tokens, width), BF16),
            pltpu.VMEM((PAD + tokens, width), BF16),
            pltpu.VMEM((tokens, width), BF16),
            pltpu.VMEM((heads, tokens, dim), BF16),
            pltpu.VMEM((heads, tokens, dim), BF16),
            pltpu.VMEM((heads, dim, dim), F32),
            pltpu.VMEM((heads, dim, dim), BF16),
            pltpu.VMEM((heads // 2, dim, dim), F32),
            pltpu.VMEM((heads // 2, dim, dim), BF16),
            pltpu.VMEM((quarter, dim, dim), F32),
            pltpu.VMEM((bits - 2, quarter, dim, dim), BF16),
            pltpu.VMEM((bits, heads, dim, dim), BF16),
            pltpu.VMEM((heads, tokens, dim), F32),
            pltpu.VMEM((heads, tokens, 8), F32),
            pltpu.SemaphoreType.DMA((3,)),
            pltpu.SemaphoreType.DMA((copies,)),
            pltpu.SemaphoreType.DMA((copies,)),
        ],
        compiler_params=pltpu.CompilerParams(
            collective_id=0, has_side_effects=True, vmem_limit_bytes=56 * 2**20
        ),
    )(
        query_rows, key_rows, value_rows, conv_taps, level_table.transpose(1, 2, 0),
        table_index.reshape(1, tokens), level_columns,
    )


def solution(mesh):
    rows = P(("groups", "ctx"), None)
    return jax.shard_map(
        on_device,
        mesh=mesh,
        in_specs=(rows, rows, rows, P(), P(), P(("groups", "ctx")), rows),
        out_specs=rows,
        check_vma=False,
    )
```

```python
import functools
import math

import jax
import jax.numpy as jnp
from jax import lax
from jax.experimental import pallas as pl
from jax.experimental.pallas import tpu as pltpu
from jax.sharding import PartitionSpec as P

F32 = jnp.float32
BF16 = jnp.bfloat16
PAD = 16


def level_factors(levels, block_len, head_dim):
    inv_root = 1.0 / math.sqrt(head_dim)
    factors = [inv_root / math.sqrt(block_len)]
    for level_pos in range(1, levels):
        factors.append(inv_root / math.sqrt(block_len * 2 ** (level_pos - 1)))
    return factors


def kernel(
    bits, heads, dim, q_hbm, k_hbm, v_hbm, taps_ref, table_ref, index_ref, cols_ref,
    out_ref, q_v, k_v, v_v, qc, kc, st_f, st_b, half_f, half_b, quart_f, quart_b,
    buck, acc, coef, load_sem, send_sem, recv_sem,
):
    tokens = q_hbm.shape[0]
    n = 2**bits
    group = lax.axis_index("groups")
    pos = lax.axis_index("ctx")
    bit = [(pos // 2**b) % 2 for b in range(bits)]
    partner = [pos + 2**b * (1 - 2 * bit[b]) for b in range(bits)]
    quarter = heads // 4
    half = heads // 2
    piece = quarter // 2

    loads = [
        pltpu.make_async_copy(src, dst.at[pl.ds(start, tokens)], load_sem.at[i])
        for i, (src, dst, start) in enumerate(((k_hbm, k_v, PAD), (v_hbm, v_v, 0), (q_hbm, q_v, PAD)))
    ]
    for load in loads:
        load.start()

    barrier = pltpu.get_barrier_semaphore()

    def greet(other):
        pl.semaphore_signal(
            barrier, inc=1, device_id=(group, other), device_id_type=pl.DeviceIdType.MESH
        )

    for b in range(bits):
        greet(partner[b])

    @pl.when(pos > 0)
    def _():
        greet(pos - 1)

    @pl.when(pos < n - 1)
    def _():
        greet(pos + 1)

    ends = (pos == 0).astype(jnp.int32) + (pos == n - 1).astype(jnp.int32)
    pl.semaphore_wait(barrier, bits + 2 - ends)

    def remote(i, src, dst, other):
        return pltpu.make_async_remote_copy(
            src_ref=src, dst_ref=dst, send_sem=send_sem.at[i], recv_sem=recv_sem.at[i],
            device_id=(group, other), device_id_type=pl.DeviceIdType.MESH,
        )

    started = []

    def send(copy, when=None):
        started.append((copy, when))
        if when is None:
            copy.start()
        else:
            pl.when(when)(copy.start)

    def wait(copy, when=None):
        if when is None:
            copy.wait_recv()
        else:
            pl.when(when)(copy.wait_recv)

    rims = []
    for i, (src, dst) in enumerate(((k_hbm, k_v), (q_hbm, q_v))):
        rim = remote(i, src.at[pl.ds(tokens - PAD, PAD)], dst.at[pl.ds(0, PAD)], pos + 1)
        send(rim, pos < n - 1)
        rims.append(rim)

    def finish_rim(i, ref):
        wait(rims[i], pos > 0)

        @pl.when(pos == 0)
        def _():
            ref[pl.ds(0, PAD), :] = jnp.zeros((PAD, ref.shape[1]), BF16)

    def lanes(h):
        return pl.ds(pl.multiple_of(h * dim, dim), dim)

    def conv(ref, which, h):
        rows = ref[:, lanes(h)].astype(F32)
        taps = taps_ref[which, :, lanes(h)]
        count = taps.shape[0]
        total = taps[count - 1 : count] * rows[PAD:]
        for back in range(1, count):
            total = total + taps[count - 1 - back : count - back] * pltpu.roll(rows, back, 0)[PAD:]
        return (0.5 * total * (1.0 + jnp.tanh(0.5 * total))).astype(BF16)

    def loop(first, count, step, one):
        def body(i, carry):
            stores = [one(first + i * step + u) for u in range(step)]
            for group_of in stores:
                for ref, at, value in group_of:
                    ref[at] = value
            return carry

        lax.fori_loop(0, count // step, body, 0)

    def state_one(h):
        key = conv(k_v, 1, h)
        state = lax.dot_general(
            key, v_v[:, lanes(h)], (((0,), (0,)), ((), ())), preferred_element_type=F32
        )
        return (kc, h, key), (st_f, h, state), (st_b, h, state.astype(BF16))

    own_half = bit[0] * half
    other_half = (1 - bit[0]) * half
    own_quart = own_half + bit[1] * quarter
    other_quart = own_half + (1 - bit[1]) * quarter

    def coefficients():
        table = table_ref[...]
        levels, _, rows = table.shape
        factors = level_factors(levels, tokens, dim)
        head_id = lax.broadcasted_iota(jnp.int32, (heads * 8, heads), 1)
        lane_id = lax.broadcasted_iota(jnp.int32, (heads * 8, heads), 0)
        leading = lax.broadcasted_iota(jnp.int32, table.shape, 0)
        mixed = jnp.zeros((heads * 8, rows), F32)
        for level in range(bits + 1):
            column = jnp.sum(jnp.where(leading == cols_ref[0, level], table, 0.0), axis=0)
            place = (lane_id == head_id * 8 + level).astype(F32)
            mixed = mixed + jnp.dot(
                place, column * factors[level],
                precision=lax.Precision.HIGHEST, preferred_element_type=F32,
            )
        hot = (lax.broadcasted_iota(jnp.int32, (rows, tokens), 0) == index_ref[...]).astype(F32)
        weights = lax.dot_general(
            hot.T, mixed, (((1,), (1,)), ((), ())),
            precision=lax.Precision.HIGHEST, preferred_element_type=F32,
        )
        for h in range(heads):
            coef[h] = weights[:, h * 8 : h * 8 + 8]

    coefficients()
    loads[0].wait()
    loads[1].wait()
    finish_rim(0, k_v)
    firsts = [
        other_half + (1 - bit[1]) * quarter, other_half + bit[1] * quarter, other_quart, own_quart
    ]
    pair = []
    for i, first in enumerate(firsts):
        loop(first, quarter, 2, state_one)
        heads_i = pl.ds(first, quarter)
        copy = remote(2 + i, st_b.at[heads_i], buck.at[0, heads_i], partner[0])
        send(copy, None if i < 2 else bit[0] == 0)
        pair.append(copy)

    for i in range(2):
        wait(pair[i])

    def half_body(i, carry):
        h = own_half + i
        total = st_f[h] + buck[0, h].astype(F32)
        half_f[i] = total
        half_b[i] = total.astype(BF16)
        return carry

    lax.fori_loop(0, half, half_body, 0)
    shares = []
    for i, (inner, first, count, when) in enumerate((
        ((1 - bit[1]) * quarter, other_quart, piece, None),
        ((1 - bit[1]) * quarter + piece, other_quart + piece, piece, None),
        (bit[1] * quarter, own_quart, quarter, bit[1] == 0),
    )):
        copy = remote(
            6 + i, half_b.at[pl.ds(inner, count)], buck.at[1, pl.ds(first, count)], partner[1]
        )
        send(copy, when)
        shares.append(copy)

    causal = lax.broadcasted_iota(jnp.int32, (tokens, tokens), 0) >= lax.broadcasted_iota(
        jnp.int32, (tokens, tokens), 1
    )

    def local_one(h):
        query = conv(q_v, 0, h)
        score = lax.dot_general(
            query, kc[h], (((1,), (1,)), ((), ())), preferred_element_type=F32
        )
        score = jnp.where(causal, score, 0.0).astype(BF16)
        read = jnp.dot(score, v_v[:, lanes(h)], preferred_element_type=F32)
        return (qc, h, query), (acc, h, read * coef[h][:, 0:1])

    def local(part):
        loop(part * quarter, quarter, 2, local_one)

    loads[2].wait()
    finish_rim(1, q_v)
    base = 10

    def stage(b, i, part, ref_from, first, other, when):
        copy = remote(
            base + 8 * (b - 2) + 2 * i + part,
            ref_from, buck.at[b, pl.ds(first + part * piece, piece)], other,
        )
        send(copy, when)
        return copy

    def exchange(b, part):
        return stage(
            b, 0, part, quart_b.at[b - 2, pl.ds(part * piece, piece)], own_quart,
            partner[b], None if b < last else bit[b] == 0,
        )

    def pass_on(b, i, part, first, other):
        here = buck.at[b, pl.ds(first + part * piece, piece)]
        return stage(b, i, part, here, first, other, bit[b] == 1)

    last = bits - 1

    def plane(part):
        def body(i, carry):
            total = half_f[bit[1] * quarter + i] + buck[1, own_quart + i].astype(F32)
            quart_f[i] = total
            quart_b[0, i] = total.astype(BF16)
            return carry

        wait(shares[part])
        lax.fori_loop(part * piece, (part + 1) * piece, body, 0)
        return exchange(2, part)

    local(0)
    first_hop = plane(0)
    local(1)
    hops = {2: [first_hop, plane(1)]}

    wait(shares[2], bit[1] == 1)
    over = remote(
        9, buck.at[1, pl.ds(own_half, half)], buck.at[1, pl.ds(own_half, half)], partner[0]
    )
    send(over, bit[1] == 1)
    local(2)

    def level_term(b, h):
        read = jnp.dot(qc[h], buck[b, h], preferred_element_type=F32)
        return acc[h] + read * coef[h][:, b + 1 : b + 2]

    def read_level(b):
        @pl.when(bit[b] == 1)
        def _():
            loop(0, heads, 4, lambda h: ((acc, h, level_term(b, h)),))

    for b in range(2, last):
        across, near, far, onward = [], [], [], []
        for part in range(2):
            wait(hops[b][part])

            def more_body(i, carry, b=b):
                total = quart_f[i] + buck[b, own_quart + i].astype(F32)
                quart_f[i] = total
                quart_b[b - 1, i] = total.astype(BF16)
                return carry

            lax.fori_loop(part * piece, (part + 1) * piece, more_body, 0)
            onward.append(exchange(b + 1, part))
            across.append(pass_on(b, 1, part, own_quart, partner[1]))
            near.append(pass_on(b, 2, part, own_quart, partner[0]))
            if b == 2 and part == 0:
                local(3)
        hops[b + 1] = onward
        if b == 2:
            wait(pair[2], bit[0] == 1)
            wait(pair[3], bit[0] == 1)
            read_level(0)
        for part in range(2):
            wait(across[part], bit[b] == 1)
            far.append(pass_on(b, 3, part, other_quart, partner[0]))
        if b == 2:
            wait(over, bit[1] == 1)
            read_level(1)
        for copy in near + far:
            wait(copy, bit[b] == 1)
        read_level(b)

    def finish(first):
        @pl.when(bit[last] == 1)
        def _():
            loop(
                first, piece, 4,
                lambda h: (
                    (out_ref, (slice(None), lanes(h)), level_term(last, h).astype(BF16)),
                ),
            )

    across, near, far = [], [], []
    near_quart = other_half + bit[1] * quarter
    far_quart = other_half + (1 - bit[1]) * quarter
    for part in range(2):
        wait(hops[last][part], bit[last] == 1)
        across.append(pass_on(last, 1, part, own_quart, partner[1]))
        near.append(pass_on(last, 2, part, own_quart, partner[0]))
        finish(own_quart + part * piece)
    wait(near[0], bit[last] == 1)
    finish(near_quart)
    for part in range(2):
        wait(across[part], bit[last] == 1)
        far.append(pass_on(last, 3, part, other_quart, partner[0]))
        finish(other_quart + part * piece)
        if part == 0:
            wait(near[1], bit[last] == 1)
            finish(near_quart + piece)
    for part in range(2):
        wait(far[part], bit[last] == 1)
        finish(far_quart + part * piece)

    @pl.when(bit[last] == 0)
    def _():
        loop(0, heads, 4, lambda h: ((out_ref, (slice(None), lanes(h)), acc[h].astype(BF16)),))

    for copy, when in started:
        if when is None:
            copy.wait_send()
        else:
            pl.when(when)(copy.wait_send)


def on_device(query_rows, key_rows, value_rows, conv_taps, level_table, table_index, level_columns):
    tokens, width = query_rows.shape
    heads = level_table.shape[2]
    dim = width // heads
    bits = lax.axis_size("ctx").bit_length() - 1
    quarter = heads // 4
    vmem = pl.BlockSpec(memory_space=pltpu.VMEM)
    hbm = pl.BlockSpec(memory_space=pl.ANY)
    copies = 10 + 8 * (bits - 2)
    return pl.pallas_call(
        functools.partial(kernel, bits, heads, dim),
        out_shape=jax.ShapeDtypeStruct((tokens, width), BF16),
        in_specs=[hbm, hbm, hbm, vmem, vmem, vmem, pl.BlockSpec(memory_space=pltpu.SMEM)],
        out_specs=vmem,
        scratch_shapes=[
            pltpu.VMEM((PAD + tokens, width), BF16),
            pltpu.VMEM((PAD + tokens, width), BF16),
            pltpu.VMEM((tokens, width), BF16),
            pltpu.VMEM((heads, tokens, dim), BF16),
            pltpu.VMEM((heads, tokens, dim), BF16),
            pltpu.VMEM((heads, dim, dim), F32),
            pltpu.VMEM((heads, dim, dim), BF16),
            pltpu.VMEM((heads // 2, dim, dim), F32),
            pltpu.VMEM((heads // 2, dim, dim), BF16),
            pltpu.VMEM((quarter, dim, dim), F32),
            pltpu.VMEM((bits - 2, quarter, dim, dim), BF16),
            pltpu.VMEM((bits, heads, dim, dim), BF16),
            pltpu.VMEM((heads, tokens, dim), F32),
            pltpu.VMEM((heads, tokens, 8), F32),
            pltpu.SemaphoreType.DMA((3,)),
            pltpu.SemaphoreType.DMA((copies,)),
            pltpu.SemaphoreType.DMA((copies,)),
        ],
        compiler_params=pltpu.CompilerParams(
            collective_id=0, has_side_effects=True, vmem_limit_bytes=56 * 2**20
        ),
    )(
        query_rows, key_rows, value_rows, conv_taps, level_table.transpose(1, 2, 0),
        table_index.reshape(1, tokens), level_columns,
    )


def solution(mesh):
    rows = P(("groups", "ctx"), None)
    return jax.shard_map(
        on_device,
        mesh=mesh,
        in_specs=(rows, rows, rows, P(), P(), P(("groups", "ctx")), rows),
        out_specs=rows,
        check_vma=False,
    )
```

```python
import functools
import math

import jax
import jax.numpy as jnp
from jax import lax
from jax.experimental import pallas as pl
from jax.experimental.pallas import tpu as pltpu
from jax.sharding import PartitionSpec as P

F32 = jnp.float32
BF16 = jnp.bfloat16
PAD = 16


def level_factors(levels, block_len, head_dim):
    inv_root = 1.0 / math.sqrt(head_dim)
    factors = [inv_root / math.sqrt(block_len)]
    for level_pos in range(1, levels):
        factors.append(inv_root / math.sqrt(block_len * 2 ** (level_pos - 1)))
    return factors


def kernel(
    bits, heads, dim, q_hbm, k_hbm, v_hbm, taps_ref, table_ref, index_ref, cols_ref,
    out_ref, q_v, k_v, v_v, qc, kc, st_f, st_b, half_f, half_b, quart_f, quart_b,
    buck, acc, coef, load_sem, send_sem, recv_sem,
):
    tokens = q_hbm.shape[0]
    n = 2**bits
    group = lax.axis_index("groups")
    pos = lax.axis_index("ctx")
    bit = [(pos // 2**b) % 2 for b in range(bits)]
    partner = [pos + 2**b * (1 - 2 * bit[b]) for b in range(bits)]
    quarter = heads // 4
    half = heads // 2
    piece = quarter // 2

    loads = [
        pltpu.make_async_copy(src, dst.at[pl.ds(start, tokens)], load_sem.at[i])
        for i, (src, dst, start) in enumerate(((k_hbm, k_v, PAD), (v_hbm, v_v, 0), (q_hbm, q_v, PAD)))
    ]
    for load in loads:
        load.start()

    barrier = pltpu.get_barrier_semaphore()

    def greet(other):
        pl.semaphore_signal(
            barrier, inc=1, device_id=(group, other), device_id_type=pl.DeviceIdType.MESH
        )

    for b in range(bits):
        greet(partner[b])

    @pl.when(pos > 0)
    def _():
        greet(pos - 1)

    @pl.when(pos < n - 1)
    def _():
        greet(pos + 1)

    ends = (pos == 0).astype(jnp.int32) + (pos == n - 1).astype(jnp.int32)
    pl.semaphore_wait(barrier, bits + 2 - ends)

    def remote(i, src, dst, other):
        return pltpu.make_async_remote_copy(
            src_ref=src, dst_ref=dst, send_sem=send_sem.at[i], recv_sem=recv_sem.at[i],
            device_id=(group, other), device_id_type=pl.DeviceIdType.MESH,
        )

    started = []

    def send(copy, when=None):
        started.append((copy, when))
        if when is None:
            copy.start()
        else:
            pl.when(when)(copy.start)

    def wait(copy, when=None):
        if when is None:
            copy.wait_recv()
        else:
            pl.when(when)(copy.wait_recv)

    rims = []
    for i, (src, dst) in enumerate(((k_hbm, k_v), (q_hbm, q_v))):
        rim = remote(i, src.at[pl.ds(tokens - PAD, PAD)], dst.at[pl.ds(0, PAD)], pos + 1)
        send(rim, pos < n - 1)
        rims.append(rim)

    def finish_rim(i, ref):
        wait(rims[i], pos > 0)

        @pl.when(pos == 0)
        def _():
            ref[pl.ds(0, PAD), :] = jnp.zeros((PAD, ref.shape[1]), BF16)

    def lanes(h):
        return pl.ds(pl.multiple_of(h * dim, dim), dim)

    def conv(ref, which, h):
        rows = ref[:, lanes(h)].astype(F32)
        taps = taps_ref[which, :, lanes(h)]
        count = taps.shape[0]
        total = taps[count - 1 : count] * rows[PAD:]
        for back in range(1, count):
            total = total + taps[count - 1 - back : count - back] * pltpu.roll(rows, back, 0)[PAD:]
        return (0.5 * total * (1.0 + jnp.tanh(0.5 * total))).astype(BF16)

    def loop(first, count, step, one):
        def body(i, carry):
            stores = [one(first + i * step + u) for u in range(step)]
            for group_of in stores:
                for ref, at, value in group_of:
                    ref[at] = value
            return carry

        lax.fori_loop(0, count // step, body, 0)

    def state_one(h):
        key = conv(k_v, 1, h)
        state = lax.dot_general(
            key, v_v[:, lanes(h)], (((0,), (0,)), ((), ())), preferred_element_type=F32
        )
        return (kc, h, key), (st_f, h, state), (st_b, h, state.astype(BF16))

    own_half = bit[0] * half
    other_half = (1 - bit[0]) * half
    own_quart = own_half + bit[1] * quarter
    other_quart = own_half + (1 - bit[1]) * quarter

    def coefficients():
        table = table_ref[...]
        levels, _, rows = table.shape
        factors = level_factors(levels, tokens, dim)
        head_id = lax.broadcasted_iota(jnp.int32, (heads * 8, heads), 1)
        lane_id = lax.broadcasted_iota(jnp.int32, (heads * 8, heads), 0)
        leading = lax.broadcasted_iota(jnp.int32, table.shape, 0)
        mixed = jnp.zeros((heads * 8, rows), F32)
        for level in range(bits + 1):
            column = jnp.sum(jnp.where(leading == cols_ref[0, level], table, 0.0), axis=0)
            place = (lane_id == head_id * 8 + level).astype(F32)
            mixed = mixed + jnp.dot(
                place, column * factors[level],
                precision=lax.Precision.HIGHEST, preferred_element_type=F32,
            )
        hot = (lax.broadcasted_iota(jnp.int32, (rows, tokens), 0) == index_ref[...]).astype(F32)
        weights = lax.dot_general(
            hot.T, mixed, (((1,), (1,)), ((), ())),
            precision=lax.Precision.HIGHEST, preferred_element_type=F32,
        )
        for h in range(heads):
            coef[h] = weights[:, h * 8 : h * 8 + 8]

    coefficients()
    loads[0].wait()
    loads[1].wait()
    finish_rim(0, k_v)
    firsts = [
        other_half + (1 - bit[1]) * quarter, other_half + bit[1] * quarter, other_quart, own_quart
    ]
    pair = []
    for i, first in enumerate(firsts):
        loop(first, quarter, 4, state_one)
        heads_i = pl.ds(first, quarter)
        copy = remote(2 + i, st_b.at[heads_i], buck.at[0, heads_i], partner[0])
        send(copy, None if i < 2 else bit[0] == 0)
        pair.append(copy)

    for i in range(2):
        wait(pair[i])

    def half_body(i, carry):
        h = own_half + i
        total = st_f[h] + buck[0, h].astype(F32)
        half_f[i] = total
        half_b[i] = total.astype(BF16)
        return carry

    lax.fori_loop(0, half, half_body, 0)
    shares = []
    for i, (inner, first, count, when) in enumerate((
        ((1 - bit[1]) * quarter, other_quart, piece, None),
        ((1 - bit[1]) * quarter + piece, other_quart + piece, piece, None),
        (bit[1] * quarter, own_quart, quarter, bit[1] == 0),
    )):
        copy = remote(
            6 + i, half_b.at[pl.ds(inner, count)], buck.at[1, pl.ds(first, count)], partner[1]
        )
        send(copy, when)
        shares.append(copy)

    causal = lax.broadcasted_iota(jnp.int32, (tokens, tokens), 0) >= lax.broadcasted_iota(
        jnp.int32, (tokens, tokens), 1
    )

    def local_one(h):
        query = conv(q_v, 0, h)
        score = lax.dot_general(
            query, kc[h], (((1,), (1,)), ((), ())), preferred_element_type=F32
        )
        score = jnp.where(causal, score, 0.0).astype(BF16)
        read = jnp.dot(score, v_v[:, lanes(h)], preferred_element_type=F32)
        return (qc, h, query), (acc, h, read * coef[h][:, 0:1])

    def local(part):
        loop(part * quarter, quarter, 4, local_one)

    loads[2].wait()
    finish_rim(1, q_v)
    base = 10

    def stage(b, i, part, ref_from, first, other, when):
        copy = remote(
            base + 8 * (b - 2) + 2 * i + part,
            ref_from, buck.at[b, pl.ds(first + part * piece, piece)], other,
        )
        send(copy, when)
        return copy

    def exchange(b, part):
        return stage(
            b, 0, part, quart_b.at[b - 2, pl.ds(part * piece, piece)], own_quart,
            partner[b], None if b < last else bit[b] == 0,
        )

    def pass_on(b, i, part, first, other):
        here = buck.at[b, pl.ds(first + part * piece, piece)]
        return stage(b, i, part, here, first, other, bit[b] == 1)

    last = bits - 1

    def plane(part):
        def body(i, carry):
            total = half_f[bit[1] * quarter + i] + buck[1, own_quart + i].astype(F32)
            quart_f[i] = total
            quart_b[0, i] = total.astype(BF16)
            return carry

        wait(shares[part])
        lax.fori_loop(part * piece, (part + 1) * piece, body, 0)
        return exchange(2, part)

    local(0)
    first_hop = plane(0)
    local(1)
    hops = {2: [first_hop, plane(1)]}

    wait(shares[2], bit[1] == 1)
    over = remote(
        9, buck.at[1, pl.ds(own_half, half)], buck.at[1, pl.ds(own_half, half)], partner[0]
    )
    send(over, bit[1] == 1)
    local(2)

    def level_term(b, h):
        read = jnp.dot(qc[h], buck[b, h], preferred_element_type=F32)
        return acc[h] + read * coef[h][:, b + 1 : b + 2]

    def read_level(b):
        @pl.when(bit[b] == 1)
        def _():
            loop(0, heads, 4, lambda h: ((acc, h, level_term(b, h)),))

    for b in range(2, last):
        across, near, far, onward = [], [], [], []
        for part in range(2):
            wait(hops[b][part])

            def more_body(i, carry, b=b):
                total = quart_f[i] + buck[b, own_quart + i].astype(F32)
                quart_f[i] = total
                quart_b[b - 1, i] = total.astype(BF16)
                return carry

            lax.fori_loop(part * piece, (part + 1) * piece, more_body, 0)
            onward.append(exchange(b + 1, part))
            across.append(pass_on(b, 1, part, own_quart, partner[1]))
            near.append(pass_on(b, 2, part, own_quart, partner[0]))
            if b == 2 and part == 0:
                local(3)
        hops[b + 1] = onward
        if b == 2:
            wait(pair[2], bit[0] == 1)
            wait(pair[3], bit[0] == 1)
            read_level(0)
        for part in range(2):
            wait(across[part], bit[b] == 1)
            far.append(pass_on(b, 3, part, other_quart, partner[0]))
        if b == 2:
            wait(over, bit[1] == 1)
            read_level(1)
        for copy in near + far:
            wait(copy, bit[b] == 1)
        read_level(b)

    def finish(first):
        @pl.when(bit[last] == 1)
        def _():
            loop(
                first, piece, 4,
                lambda h: (
                    (out_ref, (slice(None), lanes(h)), level_term(last, h).astype(BF16)),
                ),
            )

    across, near, far = [], [], []
    near_quart = other_half + bit[1] * quarter
    far_quart = other_half + (1 - bit[1]) * quarter
    for part in range(2):
        wait(hops[last][part], bit[last] == 1)
        across.append(pass_on(last, 1, part, own_quart, partner[1]))
        near.append(pass_on(last, 2, part, own_quart, partner[0]))
        finish(own_quart + part * piece)
    wait(near[0], bit[last] == 1)
    finish(near_quart)
    for part in range(2):
        wait(across[part], bit[last] == 1)
        far.append(pass_on(last, 3, part, other_quart, partner[0]))
        finish(other_quart + part * piece)
        if part == 0:
            wait(near[1], bit[last] == 1)
            finish(near_quart + piece)
    for part in range(2):
        wait(far[part], bit[last] == 1)
        finish(far_quart + part * piece)

    @pl.when(bit[last] == 0)
    def _():
        loop(0, heads, 4, lambda h: ((out_ref, (slice(None), lanes(h)), acc[h].astype(BF16)),))

    for copy, when in started:
        if when is None:
            copy.wait_send()
        else:
            pl.when(when)(copy.wait_send)


def on_device(query_rows, key_rows, value_rows, conv_taps, level_table, table_index, level_columns):
    tokens, width = query_rows.shape
    heads = level_table.shape[2]
    dim = width // heads
    bits = lax.axis_size("ctx").bit_length() - 1
    quarter = heads // 4
    vmem = pl.BlockSpec(memory_space=pltpu.VMEM)
    hbm = pl.BlockSpec(memory_space=pl.ANY)
    copies = 10 + 8 * (bits - 2)
    return pl.pallas_call(
        functools.partial(kernel, bits, heads, dim),
        out_shape=jax.ShapeDtypeStruct((tokens, width), BF16),
        in_specs=[hbm, hbm, hbm, vmem, vmem, vmem, pl.BlockSpec(memory_space=pltpu.SMEM)],
        out_specs=vmem,
        scratch_shapes=[
            pltpu.VMEM((PAD + tokens, width), BF16),
            pltpu.VMEM((PAD + tokens, width), BF16),
            pltpu.VMEM((tokens, width), BF16),
            pltpu.VMEM((heads, tokens, dim), BF16),
            pltpu.VMEM((heads, tokens, dim), BF16),
            pltpu.VMEM((heads, dim, dim), F32),
            pltpu.VMEM((heads, dim, dim), BF16),
            pltpu.VMEM((heads // 2, dim, dim), F32),
            pltpu.VMEM((heads // 2, dim, dim), BF16),
            pltpu.VMEM((quarter, dim, dim), F32),
            pltpu.VMEM((bits - 2, quarter, dim, dim), BF16),
            pltpu.VMEM((bits, heads, dim, dim), BF16),
            pltpu.VMEM((heads, tokens, dim), F32),
            pltpu.VMEM((heads, tokens, 8), F32),
            pltpu.SemaphoreType.DMA((3,)),
            pltpu.SemaphoreType.DMA((copies,)),
            pltpu.SemaphoreType.DMA((copies,)),
        ],
        compiler_params=pltpu.CompilerParams(
            collective_id=0, has_side_effects=True, vmem_limit_bytes=56 * 2**20
        ),
    )(
        query_rows, key_rows, value_rows, conv_taps, level_table.transpose(1, 2, 0),
        table_index.reshape(1, tokens), level_columns,
    )


def solution(mesh):
    rows = P(("groups", "ctx"), None)
    return jax.shard_map(
        on_device,
        mesh=mesh,
        in_specs=(rows, rows, rows, P(), P(), P(("groups", "ctx")), rows),
        out_specs=rows,
        check_vma=False,
    )
```

```python
import functools
import math

import jax
import jax.numpy as jnp
from jax import lax
from jax.experimental import pallas as pl
from jax.experimental.pallas import tpu as pltpu
from jax.sharding import PartitionSpec as P

F32 = jnp.float32
BF16 = jnp.bfloat16
PAD = 16


def level_factors(levels, block_len, head_dim):
    inv_root = 1.0 / math.sqrt(head_dim)
    factors = [inv_root / math.sqrt(block_len)]
    for level_pos in range(1, levels):
        factors.append(inv_root / math.sqrt(block_len * 2 ** (level_pos - 1)))
    return factors


def kernel(
    bits, heads, dim, q_hbm, k_hbm, v_hbm, taps_ref, table_ref, index_ref, cols_ref,
    out_ref, q_v, k_v, v_v, qc, kc, st_f, st_b, half_f, half_b, quart_f, quart_b,
    buck, acc, coef, load_sem, send_sem, recv_sem,
):
    tokens = q_hbm.shape[0]
    n = 2**bits
    group = lax.axis_index("groups")
    pos = lax.axis_index("ctx")
    bit = [(pos // 2**b) % 2 for b in range(bits)]
    partner = [pos + 2**b * (1 - 2 * bit[b]) for b in range(bits)]
    quarter = heads // 4
    half = heads // 2
    piece = quarter // 2

    loads = [
        pltpu.make_async_copy(src, dst.at[pl.ds(start, tokens)], load_sem.at[i])
        for i, (src, dst, start) in enumerate(((k_hbm, k_v, PAD), (v_hbm, v_v, 0), (q_hbm, q_v, PAD)))
    ]
    for load in loads:
        load.start()

    barrier = pltpu.get_barrier_semaphore()

    def greet(other):
        pl.semaphore_signal(
            barrier, inc=1, device_id=(group, other), device_id_type=pl.DeviceIdType.MESH
        )

    for b in range(bits):
        greet(partner[b])

    @pl.when(pos > 0)
    def _():
        greet(pos - 1)

    @pl.when(pos < n - 1)
    def _():
        greet(pos + 1)

    ends = (pos == 0).astype(jnp.int32) + (pos == n - 1).astype(jnp.int32)
    pl.semaphore_wait(barrier, bits + 2 - ends)

    def remote(i, src, dst, other):
        return pltpu.make_async_remote_copy(
            src_ref=src, dst_ref=dst, send_sem=send_sem.at[i], recv_sem=recv_sem.at[i],
            device_id=(group, other), device_id_type=pl.DeviceIdType.MESH,
        )

    started = []

    def send(copy, when=None):
        started.append((copy, when))
        if when is None:
            copy.start()
        else:
            pl.when(when)(copy.start)

    def wait(copy, when=None):
        if when is None:
            copy.wait_recv()
        else:
            pl.when(when)(copy.wait_recv)

    rims = []
    for i, (src, dst) in enumerate(((k_hbm, k_v), (q_hbm, q_v))):
        rim = remote(i, src.at[pl.ds(tokens - PAD, PAD)], dst.at[pl.ds(0, PAD)], pos + 1)
        send(rim, pos < n - 1)
        rims.append(rim)

    def finish_rim(i, ref):
        wait(rims[i], pos > 0)

        @pl.when(pos == 0)
        def _():
            ref[pl.ds(0, PAD), :] = jnp.zeros((PAD, ref.shape[1]), BF16)

    def lanes(h):
        return pl.ds(pl.multiple_of(h * dim, dim), dim)

    def conv(ref, which, h):
        rows = ref[:, lanes(h)].astype(F32)
        taps = taps_ref[which, :, lanes(h)]
        count = taps.shape[0]
        total = taps[count - 1 : count] * rows[PAD:]
        for back in range(1, count):
            total = total + taps[count - 1 - back : count - back] * pltpu.roll(rows, back, 0)[PAD:]
        return (0.5 * total * (1.0 + jnp.tanh(0.5 * total))).astype(BF16)

    def loop(first, count, step, one):
        def body(i, carry):
            stores = [one(first + i * step + u) for u in range(step)]
            for group_of in stores:
                for ref, at, value in group_of:
                    ref[at] = value
            return carry

        lax.fori_loop(0, count // step, body, 0)

    def state_one(h):
        key = conv(k_v, 1, h)
        state = lax.dot_general(
            key, v_v[:, lanes(h)], (((0,), (0,)), ((), ())), preferred_element_type=F32
        )
        return (kc, h, key), (st_f, h, state), (st_b, h, state.astype(BF16))

    own_half = bit[0] * half
    other_half = (1 - bit[0]) * half
    own_quart = own_half + bit[1] * quarter
    other_quart = own_half + (1 - bit[1]) * quarter

    def coefficients():
        table = table_ref[...]
        levels, _, rows = table.shape
        factors = level_factors(levels, tokens, dim)
        head_id = lax.broadcasted_iota(jnp.int32, (heads * 8, heads), 1)
        lane_id = lax.broadcasted_iota(jnp.int32, (heads * 8, heads), 0)
        leading = lax.broadcasted_iota(jnp.int32, table.shape, 0)
        mixed = jnp.zeros((heads * 8, rows), F32)
        for level in range(bits + 1):
            column = jnp.sum(jnp.where(leading == cols_ref[0, level], table, 0.0), axis=0)
            place = (lane_id == head_id * 8 + level).astype(F32)
            mixed = mixed + jnp.dot(
                place, column * factors[level],
                precision=lax.Precision.HIGHEST, preferred_element_type=F32,
            )
        hot = (lax.broadcasted_iota(jnp.int32, (rows, tokens), 0) == index_ref[...]).astype(F32)
        weights = lax.dot_general(
            hot.T, mixed, (((1,), (1,)), ((), ())),
            precision=lax.Precision.HIGHEST, preferred_element_type=F32,
        )
        for h in range(heads):
            coef[h] = weights[:, h * 8 : h * 8 + 8]

    coefficients()
    loads[0].wait()
    loads[1].wait()
    finish_rim(0, k_v)
    firsts = [
        other_half + (1 - bit[1]) * quarter, other_half + bit[1] * quarter, other_quart, own_quart
    ]
    pair = []

    def states(i):
        loop(firsts[i], quarter, 4, state_one)
        heads_i = pl.ds(firsts[i], quarter)
        copy = remote(2 + i, st_b.at[heads_i], buck.at[0, heads_i], partner[0])
        send(copy, None if i < 2 else bit[0] == 0)
        pair.append(copy)

    def half_body(i, carry):
        h = own_half + i
        total = st_f[h] + buck[0, h].astype(F32)
        half_f[i] = total
        half_b[i] = total.astype(BF16)
        return carry

    shares = []

    def share(inner, first, count, when):
        copy = remote(
            6 + len(shares), half_b.at[pl.ds(inner, count)],
            buck.at[1, pl.ds(first, count)], partner[1],
        )
        send(copy, when)
        shares.append(copy)

    states(0)
    states(1)
    states(2)
    wait(pair[0])
    inner = (1 - bit[1]) * quarter
    for part in range(2):
        start = inner + part * piece
        lax.fori_loop(start, start + piece, half_body, 0)
        share(start, own_half + start, piece, None)
    states(3)
    wait(pair[1])
    inner = bit[1] * quarter
    lax.fori_loop(inner, inner + quarter, half_body, 0)
    share(inner, own_quart, quarter, bit[1] == 0)

    causal = lax.broadcasted_iota(jnp.int32, (tokens, tokens), 0) >= lax.broadcasted_iota(
        jnp.int32, (tokens, tokens), 1
    )

    def local_one(h):
        query = conv(q_v, 0, h)
        score = lax.dot_general(
            query, kc[h], (((1,), (1,)), ((), ())), preferred_element_type=F32
        )
        score = jnp.where(causal, score, 0.0).astype(BF16)
        read = jnp.dot(score, v_v[:, lanes(h)], preferred_element_type=F32)
        return (qc, h, query), (acc, h, read * coef[h][:, 0:1])

    def local(part):
        loop(part * quarter, quarter, 4, local_one)

    loads[2].wait()
    finish_rim(1, q_v)
    base = 10

    def stage(b, i, part, ref_from, first, other, when):
        copy = remote(
            base + 8 * (b - 2) + 2 * i + part,
            ref_from, buck.at[b, pl.ds(first + part * piece, piece)], other,
        )
        send(copy, when)
        return copy

    def exchange(b, part):
        return stage(
            b, 0, part, quart_b.at[b - 2, pl.ds(part * piece, piece)], own_quart,
            partner[b], None if b < last else bit[b] == 0,
        )

    def pass_on(b, i, part, first, other):
        here = buck.at[b, pl.ds(first + part * piece, piece)]
        return stage(b, i, part, here, first, other, bit[b] == 1)

    last = bits - 1

    def plane(part):
        def body(i, carry):
            total = half_f[bit[1] * quarter + i] + buck[1, own_quart + i].astype(F32)
            quart_f[i] = total
            quart_b[0, i] = total.astype(BF16)
            return carry

        wait(shares[part])
        lax.fori_loop(part * piece, (part + 1) * piece, body, 0)
        return exchange(2, part)

    local(0)
    first_hop = plane(0)
    local(1)
    hops = {2: [first_hop, plane(1)]}

    wait(shares[2], bit[1] == 1)
    over = remote(
        9, buck.at[1, pl.ds(own_half, half)], buck.at[1, pl.ds(own_half, half)], partner[0]
    )
    send(over, bit[1] == 1)
    local(2)

    def level_term(b, h):
        read = jnp.dot(qc[h], buck[b, h], preferred_element_type=F32)
        return acc[h] + read * coef[h][:, b + 1 : b + 2]

    def read_level(b):
        @pl.when(bit[b] == 1)
        def _():
            loop(0, heads, 4, lambda h: ((acc, h, level_term(b, h)),))

    for b in range(2, last):
        across, near, far, onward = [], [], [], []
        for part in range(2):
            wait(hops[b][part])

            def more_body(i, carry, b=b):
                total = quart_f[i] + buck[b, own_quart + i].astype(F32)
                quart_f[i] = total
                quart_b[b - 1, i] = total.astype(BF16)
                return carry

            lax.fori_loop(part * piece, (part + 1) * piece, more_body, 0)
            onward.append(exchange(b + 1, part))
            across.append(pass_on(b, 1, part, own_quart, partner[1]))
            near.append(pass_on(b, 2, part, own_quart, partner[0]))
            if b == 2 and part == 0:
                local(3)
        hops[b + 1] = onward
        if b == 2:
            wait(pair[2], bit[0] == 1)
            wait(pair[3], bit[0] == 1)
            read_level(0)
        for part in range(2):
            wait(across[part], bit[b] == 1)
            far.append(pass_on(b, 3, part, other_quart, partner[0]))
        if b == 2:
            wait(over, bit[1] == 1)
            read_level(1)
        for copy in near + far:
            wait(copy, bit[b] == 1)
        read_level(b)

    def finish(first):
        @pl.when(bit[last] == 1)
        def _():
            loop(
                first, piece, 4,
                lambda h: (
                    (out_ref, (slice(None), lanes(h)), level_term(last, h).astype(BF16)),
                ),
            )

    across, near, far = [], [], []
    near_quart = other_half + bit[1] * quarter
    far_quart = other_half + (1 - bit[1]) * quarter
    for part in range(2):
        wait(hops[last][part], bit[last] == 1)
        across.append(pass_on(last, 1, part, own_quart, partner[1]))
        near.append(pass_on(last, 2, part, own_quart, partner[0]))
        finish(own_quart + part * piece)
    wait(near[0], bit[last] == 1)
    finish(near_quart)
    for part in range(2):
        wait(across[part], bit[last] == 1)
        far.append(pass_on(last, 3, part, other_quart, partner[0]))
        finish(other_quart + part * piece)
        if part == 0:
            wait(near[1], bit[last] == 1)
            finish(near_quart + piece)
    for part in range(2):
        wait(far[part], bit[last] == 1)
        finish(far_quart + part * piece)

    @pl.when(bit[last] == 0)
    def _():
        loop(0, heads, 4, lambda h: ((out_ref, (slice(None), lanes(h)), acc[h].astype(BF16)),))

    for copy, when in started:
        if when is None:
            copy.wait_send()
        else:
            pl.when(when)(copy.wait_send)


def on_device(query_rows, key_rows, value_rows, conv_taps, level_table, table_index, level_columns):
    tokens, width = query_rows.shape
    heads = level_table.shape[2]
    dim = width // heads
    bits = lax.axis_size("ctx").bit_length() - 1
    quarter = heads // 4
    vmem = pl.BlockSpec(memory_space=pltpu.VMEM)
    hbm = pl.BlockSpec(memory_space=pl.ANY)
    copies = 10 + 8 * (bits - 2)
    return pl.pallas_call(
        functools.partial(kernel, bits, heads, dim),
        out_shape=jax.ShapeDtypeStruct((tokens, width), BF16),
        in_specs=[hbm, hbm, hbm, vmem, vmem, vmem, pl.BlockSpec(memory_space=pltpu.SMEM)],
        out_specs=vmem,
        scratch_shapes=[
            pltpu.VMEM((PAD + tokens, width), BF16),
            pltpu.VMEM((PAD + tokens, width), BF16),
            pltpu.VMEM((tokens, width), BF16),
            pltpu.VMEM((heads, tokens, dim), BF16),
            pltpu.VMEM((heads, tokens, dim), BF16),
            pltpu.VMEM((heads, dim, dim), F32),
            pltpu.VMEM((heads, dim, dim), BF16),
            pltpu.VMEM((heads // 2, dim, dim), F32),
            pltpu.VMEM((heads // 2, dim, dim), BF16),
            pltpu.VMEM((quarter, dim, dim), F32),
            pltpu.VMEM((bits - 2, quarter, dim, dim), BF16),
            pltpu.VMEM((bits, heads, dim, dim), BF16),
            pltpu.VMEM((heads, tokens, dim), F32),
            pltpu.VMEM((heads, tokens, 8), F32),
            pltpu.SemaphoreType.DMA((3,)),
            pltpu.SemaphoreType.DMA((copies,)),
            pltpu.SemaphoreType.DMA((copies,)),
        ],
        compiler_params=pltpu.CompilerParams(
            collective_id=0, has_side_effects=True, vmem_limit_bytes=56 * 2**20
        ),
    )(
        query_rows, key_rows, value_rows, conv_taps, level_table.transpose(1, 2, 0),
        table_index.reshape(1, tokens), level_columns,
    )


def solution(mesh):
    rows = P(("groups", "ctx"), None)
    return jax.shard_map(
        on_device,
        mesh=mesh,
        in_specs=(rows, rows, rows, P(), P(), P(("groups", "ctx")), rows),
        out_specs=rows,
        check_vma=False,
    )
```
